32 devices in a mesh: groups: 2 (over y), hidden: 4 (over x, core), dp: 4 (over z).
Axes of the slice: x: 2, y: 2, z: 4, core: 2. Of those that a mesh axis runs over, the one named last changes fastest.
Arguments:
- activations: bfloat16 [3072, 16384], P(('groups', 'dp'), 'hidden'), parts along dimension 0, may hold values from -6 to 6
- response_mask: int32 [3072], P(('groups', 'dp')), parts along dimension 0, may hold values from 0 to 1, as said below
- seq_lengths: int32 [8, 8], P(('groups', 'dp')), parts along dimension 0, may hold values from 1 to 96, as said below
Outputs:
- factor: float32 [32768, 4, 4096], P(('groups', 'hidden'), None, 'dp'), parts along dimension 0
The draws below stay inside these ranges and needn't reach their ends.
There are 2 independent parts, one for each index of `groups`. The reference program is written for one: setup_inputs(seed, part) draws one part's arguments, and reference() takes and returns one part's arrays. A program takes and returns all parts, laid end to end along the dimension named above; each array names one. Nothing has to cross between parts.
Inputs may be any that keep to these rules, and one draw needn't show every extreme that they name: `seq_lengths`: each row sums to 384; its largest entry is exactly 96 and its smallest is 1. In each index of dp, one or more sequences have no token with response_mask 1, and one or more have a token with response_mask 1.
All inputs are finite; a program needn't handle non-finite values.
Results may differ from the reference program's by a relative error of at most 0.0017.
Values may be sent and summed in bfloat16 or wider, within the bound.
A program may use at most 320 MiB of HBM per device.

```python
import jax
import jax.numpy as jnp
from jax import lax

D = 16384
TOK_DEV = 384
SEQ_DEV = 8
MOST_LEN = 96
TOKENS = 1536
N_HIDDEN = 4
N_DP = 4


def packing(key):
    keys = jax.random.split(key, 4)
    longest = MOST_LEN
    first = jax.random.randint(keys[0], (N_DP,), 1, longest)
    second = jax.random.randint(keys[1], (N_DP,), 1, longest)
    third = jax.random.randint(keys[2], (N_DP,), 1, longest - 1)
    full_len = jnp.full((N_DP,), longest, jnp.int32)
    single = jnp.ones((N_DP,), jnp.int32)
    pieces = jnp.stack([full_len, first, longest - first, second, longest - second, single, third, longest - 1 - third], axis=1).astype(jnp.int32)
    slot_ids = jnp.arange(SEQ_DEV, dtype=jnp.int32)
    kinds = jnp.where(slot_ids == 0, 0, jnp.where(slot_ids == 1, 1, 2)).astype(jnp.int32)
    kinds = jnp.broadcast_to(kinds[None, :], (N_DP, SEQ_DEV))
    scores = jax.random.randint(keys[3], (N_DP, SEQ_DEV), 0, 1 << 20) * SEQ_DEV + slot_ids[None, :]
    order = jnp.argsort(scores, axis=1, stable=True)
    lengths = jnp.take_along_axis(pieces, order, axis=1)
    kinds = jnp.take_along_axis(kinds, order, axis=1)
    return (lengths.astype(jnp.int32), kinds.astype(jnp.int32))


def draw_seq_lengths(key, part):
    lengths, kinds = packing(key)
    return lengths


def draw_response_mask(key, part):
    lengths, kinds = packing(key)
    key = jax.random.fold_in(key, 11)
    keys = jax.random.split(key, 3)
    alive_bits = jax.random.randint(keys[0], (N_DP, SEQ_DEV), 0, 4) < 3
    alive = (kinds == 0) | (kinds == 2) & alive_bits
    ends = jnp.cumsum(lengths, axis=1)
    starts = ends - lengths
    places = jnp.arange(TOK_DEV, dtype=jnp.int32)
    member = (places[None, :, None] >= starts[:, None, :]) & (places[None, :, None] < ends[:, None, :])
    token_alive = jnp.any(member & alive[:, None, :], axis=2)
    coins = jax.random.randint(keys[1], (N_DP, TOK_DEV), 0, 4) < 3
    offsets = jax.random.randint(keys[2], (N_DP,), 0, MOST_LEN)
    full_start = jnp.sum(jnp.where(kinds == 0, starts, 0), axis=1)
    forced = places[None, :] == (full_start + offsets)[:, None]
    marks = token_alive & (coins | forced)
    return marks.astype(jnp.int32).reshape(TOKENS)


def steps_of(key, extent, cuts, low, largest):
    factor_of, own = 1.0, jax.random.fold_in(key, 6)
    for dim, shards_of in cuts:
        heights = jnp.exp(jax.random.uniform(jax.random.fold_in(own, dim), (shards_of,), jnp.float32, low / len(cuts), largest / len(cuts)))
        factor_of = factor_of * jnp.repeat(heights, extent[dim] // shards_of).reshape([-1 if axis == dim else 1 for axis in range(len(extent))])
    return factor_of


def centred(rng, dims, spread, bound, cuts=(), kind=jnp.bfloat16):
    entries = spread * jax.random.normal(rng, dims, jnp.float32)
    if cuts:
        entries = entries * steps_of(rng, dims, cuts, -0.22, 0.18)
    return jnp.clip(entries, -bound, bound).astype(kind)


def setup_inputs(seed: int = 0, part: int = 0) -> dict:
    seeds = jax.random.split(jax.random.key(seed), 4)
    part_splits = jax.random.split(jax.random.fold_in(seeds[3], part), 4)
    return {
        "activations": centred(part_splits[0], (TOKENS, D), 1.0, 6.0, ((0, 4), (1, 4))),
        "response_mask": draw_response_mask(jax.random.fold_in(jax.random.fold_in(seeds[3], part), 71), part),
        "seq_lengths": draw_seq_lengths(jax.random.fold_in(jax.random.fold_in(seeds[3], part), 71), part),
    }


def block_weights(flags, lengths):
    ends = jnp.cumsum(lengths)
    starts = ends - lengths
    places = jnp.arange(flags.shape[0], dtype=jnp.int32)[:, None]
    member = ((places >= starts[None, :]) & (places < ends[None, :])).astype(jnp.float32)
    marks = flags.astype(jnp.float32)
    counts = jnp.sum(member * marks[:, None], axis=0)
    inverse = 1.0 / jnp.maximum(counts, 1.0)
    return marks * jnp.sum(member * inverse[None, :], axis=1)


def reference(activations, response_mask, seq_lengths):
    flags = response_mask.reshape(N_DP, TOK_DEV)
    weight = jax.vmap(block_weights)(flags, seq_lengths).reshape(TOKENS)
    total = jnp.sum(weight)
    weighted = (weight[:, None] * activations.astype(jnp.float32)).astype(jnp.bfloat16)
    width = D // N_HIDDEN
    panels = jnp.transpose(weighted.reshape(TOKENS, N_HIDDEN, width), (1, 0, 2))

    def one_block(panel):
        return jnp.dot(panel.T, activations, preferred_element_type=jnp.float32)

    gram = lax.map(one_block, panels).reshape(D, D)
    return (gram / total).reshape(D, N_HIDDEN, width)
```

```python
import functools

import jax
import jax.numpy as jnp
from jax import lax
from jax.experimental import pallas as pl
from jax.experimental.pallas import tpu as pltpu
from jax.sharding import PartitionSpec as P


def token_weights(flags, lengths):
    ends = jnp.cumsum(lengths)
    starts = ends - lengths
    places = jnp.arange(flags.shape[0], dtype=jnp.int32)[:, None]
    member = ((places >= starts[None, :]) & (places < ends[None, :])).astype(jnp.float32)
    marks = flags.astype(jnp.float32)
    counts = jnp.sum(member * marks[:, None], axis=0)
    inverse = 1.0 / jnp.maximum(counts, 1.0)
    return marks * jnp.sum(member * inverse[None, :], axis=1)


def gram_kernel(n_hidden, n_in, place_ref, total_ref, left_ref, *rest):
    panels, out_ref, turned = rest[:n_hidden], rest[n_in], rest[n_in + 1]
    scale = 1.0 / total_ref[0]
    rows = out_ref.shape[0]
    tile = min(256, rows)

    @pl.when(pl.program_id(0) == 0)
    def _():
        for r in range(0, rows, tile):
            turned[r : r + tile, :] = left_ref[:, r : r + tile].T

    @pl.loop(0, rows // tile)
    def _(r):
        here = pl.ds(pl.multiple_of(r * tile, tile), tile)
        for k in range(n_hidden):
            acc = jnp.dot(turned[here, :], panels[k][...], preferred_element_type=jnp.float32)
            out_ref[here, k, :] = acc * scale


def gram_rows(place, total, left, panel, prev, rows):
    tokens, sub = left.shape
    n_hidden = panel.shape[1] // sub
    tile = min(256, sub)
    steps = sub // tile

    def block_of(k, j, place):
        return (0, k * steps + j)

    in_specs = [
        pl.BlockSpec(memory_space=pltpu.SMEM),
        pl.BlockSpec((tokens, sub), lambda j, place: (0, 0), pipeline_mode=pl.Buffered(1)),
    ]
    in_specs += [
        pl.BlockSpec((tokens, tile), functools.partial(block_of, k)) for k in range(n_hidden)
    ]
    operands = [place, total, left] + [panel] * n_hidden
    aliases = {}
    if prev is not None:
        in_specs.append(pl.BlockSpec(memory_space=pl.ANY))
        aliases = {len(operands): 0}
        operands.append(prev)
    return pl.pallas_call(
        functools.partial(gram_kernel, n_hidden, len(in_specs) - 2),
        out_shape=jax.ShapeDtypeStruct((rows, n_hidden, sub), jnp.float32),
        grid_spec=pltpu.PrefetchScalarGridSpec(
            num_scalar_prefetch=1,
            grid=(steps,),
            in_specs=in_specs,
            out_specs=pl.BlockSpec((sub, n_hidden, tile), lambda j, place: (place[0], 0, j)),
            scratch_shapes=[pltpu.VMEM((sub, tokens), jnp.bfloat16)],
        ),
        input_output_aliases=aliases,
        compiler_params=pltpu.CompilerParams(vmem_limit_bytes=40 * 1024 * 1024),
        cost_estimate=pl.CostEstimate(
            flops=2 * tokens * sub * n_hidden * sub,
            bytes_accessed=4 * sub * n_hidden * sub + 2 * tokens * sub * (n_hidden + 1),
            transcendentals=0,
        ),
    )(*operands)


def exchange_hidden(mine, n_hidden):
    have = {0: mine}
    step = n_hidden // 2
    while step:
        pairs = [(i, i ^ step) for i in range(n_hidden)]
        for r in list(have):
            have[r ^ step] = lax.ppermute(have[r], "hidden", pairs)
        step //= 2
    return [have[r] for r in range(n_hidden)]


def assemble_kernel(n, n_hidden, hidden_ref, *rest):
    pieces, panel, sems = rest[: n * n_hidden], rest[-2], rest[-1]
    tok, sub = pieces[0].shape
    copies = []
    for s in range(n):
        for r in range(n_hidden):
            k = lax.bitwise_xor(hidden_ref[0], jnp.int32(r))
            copies.append(
                pltpu.make_async_copy(
                    pieces[s * n_hidden + r],
                    panel.at[pl.ds(s * tok, tok), pl.ds(pl.multiple_of(k * sub, sub), sub)],
                    sems.at[s * n_hidden + r],
                )
            )
    for copy in copies:
        copy.start()
    for copy in copies:
        copy.wait()


def assemble(hidden, pieces, n, n_hidden):
    tok, sub = pieces[0].shape
    return pl.pallas_call(
        functools.partial(assemble_kernel, n, n_hidden),
        out_shape=jax.ShapeDtypeStruct((n * tok, n_hidden * sub), pieces[0].dtype),
        in_specs=[pl.BlockSpec(memory_space=pltpu.SMEM)]
        + [pl.BlockSpec(memory_space=pltpu.VMEM)] * len(pieces),
        out_specs=pl.BlockSpec(memory_space=pl.ANY),
        scratch_shapes=[pltpu.SemaphoreType.DMA((len(pieces),))],
        compiler_params=pltpu.CompilerParams(vmem_limit_bytes=24 * 1024 * 1024),
        cost_estimate=pl.CostEstimate(
            flops=0, bytes_accessed=4 * n * tok * n_hidden * sub, transcendentals=0
        ),
    )(hidden, *pieces)


def per_device(activations, response_mask, seq_lengths):
    tok, width = activations.shape
    n_hidden = lax.axis_size("hidden")
    n = lax.axis_size("dp")
    me = lax.axis_index("dp")
    sub = width // n

    weight = token_weights(response_mask, seq_lengths.reshape(-1))
    def own(c):
        return lax.dynamic_slice(activations, (0, lax.rem(c + 2 * n, n) * sub), (tok, sub))

    *mine, weight = lax.optimization_barrier([own(me + m) for m in range(n)] + [weight])
    slot_weights = [weight] + [
        lax.ppermute(weight, "dp", [(i, (i + s) % n) for i in range(n)]) for s in range(1, n)
    ]
    total = sum(jnp.sum(w) for w in slot_weights).reshape(1)

    up_pairs = [(i, i + 1) for i in range(n - 1)]
    down_pairs = [(i + 1, i) for i in range(n - 1)]
    low = [dict(enumerate(mine))] + [{} for _ in range(1, n)]
    high = [dict(enumerate(mine))] + [{} for _ in range(1, n)]
    upper = me >= n // 2

    def piece(s, p):
        a, b = p, (-p) % n
        if s == 0:
            return mine[a] if a == b else jnp.where(upper, mine[a], mine[b])

        def at(m):
            return jnp.where(me >= s, low[s][m], high[n - s][m])

        return at(a) if a == b else jnp.where(upper, at(a), at(b))

    columns, crossed, crossed_at = {}, {}, {}

    def cross(s):
        columns[s] = lax.optimization_barrier(piece(s, 0))
        crossed[s] = exchange_hidden(columns[s], n_hidden)

    cross(0)
    order = [(s, d - s) for d in range(1, 2 * n - 1) for s in range(1, n) if 0 <= d - s < n]
    window = 3
    ups, downs, waited = [], [], set()
    for i, (s, q) in enumerate(order):
        after_up = ups[i - window : i - window + 1] if i >= window else []
        after_down = downs[i - window : i - window + 1] if i >= window else []
        for slot in sorted(crossed):
            if slot not in waited and crossed_at.get(slot, 0) + 2 * window <= i + 1:
                waited.add(slot)
                after_up = after_up + crossed[slot][n_hidden // 2 : n_hidden // 2 + 1]
        m = q
        source = low[s - 1][(m + 1) % n]
        if after_up:
            source = lax.optimization_barrier([source] + after_up)[0]
        low[s][m] = lax.ppermute(source, "dp", [x for x in up_pairs if x[0] >= s - 1])
        ups.append(low[s][m])
        m = (-q) % n
        source = high[s - 1][(m - 1) % n]
        if after_down:
            source = lax.optimization_barrier([source] + after_down)[0]
        high[s][m] = lax.ppermute(source, "dp", [x for x in down_pairs if x[0] <= n - s])
        downs.append(high[s][m])
        for slot in range(1, n):
            if slot not in crossed and 0 in low[slot] and 0 in high[n - slot]:
                cross(slot)
                crossed_at[slot] = i

    hidden = lax.axis_index("hidden").astype(jnp.int32)
    spread = [x for s in range(n) for x in crossed[s]]
    panel = assemble(hidden.reshape(1), spread, n, n_hidden)

    out = None
    for p in range(n):
        left = jnp.concatenate(
            [
                (slot_weights[s][:, None] * (piece(s, p) if p else columns[s]).astype(jnp.float32)).astype(jnp.bfloat16)
                for s in range(n)
            ],
            axis=0,
        )
        chunk = lax.rem(jnp.where(upper, me + p, me + (-p) % n), n)
        place = chunk.reshape(1).astype(jnp.int32)
        out = gram_rows(place, total, left, panel, out, width)
    return out


def solution(mesh):
    placed = (P(("groups", "dp"), "hidden"), P(("groups", "dp")), P(("groups", "dp"), None))
    return jax.shard_map(
        per_device,
        mesh=mesh,
        in_specs=placed,
        out_specs=P(("groups", "hidden"), None, "dp"),
        check_vma=False,
    )
```
